256 devices in a mesh: dp: 16 (over z_lo, y), expert: 16 (over z_hi, x, core).
Axes of the slice: x: 4, y: 4, z: 8 (z_hi: 2, z_lo: 4; z = z_hi * 4 + z_lo), core: 2. Of those that a mesh axis runs over, the one named last changes fastest.
Arguments:
- tokens: bfloat16 [32768, 1024], P(('dp', 'expert')), may hold values from -6 to 6
- grad_out: bfloat16 [32768, 1024], P(('dp', 'expert')), may hold values from -3 to 3
- expert_ids: int32 [32768, 2], P(('dp', 'expert')), may hold values from 0 to 31, all different within a row; in each aligned block of 128 rows (0 to 127, 128 to 255, ...) at most 10 rows name the same one
- gate_values: bfloat16 [32768, 2], P(('dp', 'expert')), may hold values from 0.099609375 to 1
- weight_in: bfloat16 [32, 1024, 4096], P('expert', None, 'dp'), may hold values from -0.1875 to 0.1875
- weight_out: bfloat16 [32, 4096, 1024], P('expert', 'dp'), may hold values from -0.09375 to 0.09375
Outputs:
- grad_tokens: bfloat16 [32768, 1024], P(('dp', 'expert'))
- grad_gates: float32 [32768, 2], P(('dp', 'expert'))
- grad_weight_in: float32 [32, 1024, 4096], P('expert', None, 'dp')
- grad_weight_out: float32 [32, 4096, 1024], P('expert', 'dp')
The draws below stay inside these ranges and needn't reach their ends.
Inputs may be any that keep to these rules, and one draw needn't show every extreme that they name: `expert_ids`: the 2 experts of one token differ. Among the 128 tokens of one device (aligned blocks of rows in order), no expert is named more than 10 times, a bound that some block reaches.
All inputs are finite; a program needn't handle non-finite values.
Results may differ from the reference program's by a relative error of at most 0.024.
Values may be sent and summed in bfloat16 or wider, within the bound.
A program may use at most 128 MiB of HBM per device.

```python
import math
import jax
import jax.numpy as jnp
import numpy as np
from jax import lax

D = 1024
FF = 4096
TOP = 2
TOK_DEV = 128
EXPERTS = 32
CAP = 10
TOKENS = 32768
N_DP = 16
DEVICES = 256


def levels(rng, shape, cuts, low, largest):
    level = 1.0
    for axis_at, parts in cuts:
        draws = jax.random.uniform(jax.random.fold_in(jax.random.fold_in(rng, 6), axis_at), (parts,), jnp.float32, low / len(cuts), largest / len(cuts))
        level = level * jnp.repeat(jnp.exp(draws), shape[axis_at] // parts).reshape((-1,) + (1,) * (len(shape) - 1 - axis_at))
    return level


def deal_out(own_key, own, number, rows, number_of, top, reach, skew):
    ranking = jax.random.permutation(own_key, number_of)
    heavy_load, common = portions_of(number_of, rows * top, reach, skew, True), portions_of(number_of, rows * top, reach, skew, False)
    places = jnp.arange(number_of)

    def named(sizes, offset_by):
        used = int((sizes > 0).sum())
        fixed = max(1, used // 4)
        shifted = fixed + (places - fixed + offset_by * (used - fixed)) % max(1, number_of - fixed)
        return jnp.zeros((number_of,), jnp.int32).at[ranking[jnp.where(places < fixed, places, shifted)]].set(jnp.asarray(sizes, jnp.int32))

    sizes = jnp.where(number % 4 == 0, named(heavy_load, number // 4), named(common, number - number // 4 - 1))
    mixed = jax.random.permutation(jax.random.fold_in(own, 3), number_of)
    giver, sink = mixed[0:number_of // 2 * 2:2], mixed[1:number_of // 2 * 2:2]
    slack = jnp.minimum(sizes[giver] - 1, reach - sizes[sink]) // 2
    slack = jnp.where((giver == ranking[0]) | (sink == ranking[0]) | (sizes[sink] == 0), 0, jnp.maximum(slack, 0))
    shifted = jax.random.randint(jax.random.fold_in(own, 4), (number_of // 2,), 0, 1 << 20) % (slack + 1)
    sizes = sizes.at[giver].add(-shifted).at[sink].add(shifted)
    members = jnp.searchsorted(jnp.cumsum(sizes), jnp.arange(rows * top), side="right").astype(jnp.int32)
    grid = members.reshape(top, rows).T
    grid = grid[jax.random.permutation(jax.random.fold_in(own, 1), rows)]
    offset_by = jax.random.randint(jax.random.fold_in(own, 2), (rows, 1), 0, top)
    return jnp.take_along_axis(grid, (jnp.arange(top)[None, :] + offset_by) % top, axis=1)


def portions_of(count, total, bound, skew, full):
    loads = [(1 << 20) // math.isqrt(rank ** skew) + 1 for rank in range(1, count + 1)]
    largest = bound if full else min(bound, max(-(-total // count), total * loads[0] // sum(loads)))
    least = 1 if total - largest >= count - 1 else 0
    given, surplus = [largest] + [least] * (count - 1), total - largest - least * (count - 1)
    while surplus > 0:
        free = [i for i in range(1, count) if given[i] < largest] or [i for i in range(1, count) if given[i] < bound]
        mass, remaining = sum([loads[i] for i in free]), surplus
        for i in free:
            more = min(bound - given[i], max(1, remaining * loads[i] // mass), surplus)
            given[i] = given[i] + more
            surplus = surplus - more
    return np.array(given)


def noise(key, dims, scale, bound, cuts=(), kind=jnp.bfloat16):
    drawn = jax.random.normal(key, dims, jnp.float32) * scale
    if len(cuts) > 0:
        drawn = levels(key, dims, cuts, -0.22, 0.18) * drawn
    return jnp.clip(drawn, min=-bound, max=bound).astype(kind)


def setup_inputs(seed: int = 0) -> dict:
    keys = jax.random.split(jax.random.key(seed), 7)
    tokens = noise(keys[0], (TOKENS, D), 1.0, 6.0, ((0, 256),))
    grad_out = noise(keys[1], (TOKENS, D), 0.5, 3.0, ((0, 256),))
    expert_ids_keys = jax.random.split(jax.random.fold_in(keys[2], 1), TOKENS // TOK_DEV)
    expert_ids_turns = jax.random.permutation(jax.random.fold_in(keys[2], 3), TOKENS // TOK_DEV)
    expert_ids = jax.vmap(lambda own, number: deal_out(jax.random.fold_in(keys[2], 2), own, number, TOK_DEV, EXPERTS, TOP, CAP, 2))(expert_ids_keys, expert_ids_turns).reshape((TOKENS, TOP))
    gate_values = jnp.clip(0.099609375 + 0.9003906 * jax.random.uniform(keys[3], (TOKENS, TOP), jnp.float32) ** levels(keys[3], (TOKENS, TOP), ((0, 256),), -0.2, 0.2), 0.099609375, 1.0).astype(jnp.bfloat16)
    weight_in = noise(keys[4], (EXPERTS, D, FF), D ** -0.5, 0.1875, ((0, 16), (2, 16)))
    weight_out = noise(keys[5], (EXPERTS, FF, D), FF ** -0.5, 0.09375, ((0, 16), (1, 16)))
    return {"tokens": tokens, "grad_out": grad_out, "expert_ids": expert_ids, "gate_values": gate_values, "weight_in": weight_in, "weight_out": weight_out}


GELU_SCALE = 0.7978845608028654
GELU_CUBIC = 0.044715


def slot_positions(route_ids):
    flat_ids = route_ids.reshape(-1)
    onehot = (flat_ids[:, None] == jnp.arange(EXPERTS, dtype=jnp.int32)[None, :]).astype(jnp.int32)
    before = jnp.cumsum(onehot, axis=0) - onehot
    return jnp.sum(before * onehot, axis=1).astype(jnp.int32).reshape(route_ids.shape)


def dispatch_one(token_rows, grad_rows, gate_rows, route_ids):
    positions = slot_positions(route_ids)
    slot_index = (route_ids * CAP + positions).reshape(-1).astype(jnp.int32)
    source = jnp.repeat(jnp.arange(TOK_DEV, dtype=jnp.int32), TOP)
    slot_x = jnp.zeros((EXPERTS * CAP, D), token_rows.dtype).at[slot_index].set(token_rows[source])
    slot_dy = jnp.zeros((EXPERTS * CAP, D), grad_rows.dtype).at[slot_index].set(grad_rows[source])
    slot_gate = jnp.zeros((EXPERTS * CAP,), gate_rows.dtype).at[slot_index].set(gate_rows.reshape(-1))
    return slot_x, slot_dy, slot_gate, slot_index


def by_expert(table):
    tail = table.shape[2:]
    split = table.reshape((DEVICES, EXPERTS, CAP) + tail)
    return jnp.swapaxes(split, 0, 1).reshape((EXPERTS, DEVICES * CAP) + tail)


def by_device(table):
    tail = table.shape[2:]
    split = table.reshape((EXPERTS, DEVICES, CAP) + tail)
    return jnp.swapaxes(split, 0, 1).reshape((DEVICES, EXPERTS * CAP) + tail)


def expert_grads(operands):
    routed_x, routed_dy, routed_gate, expert_in, expert_out = operands
    hidden_pre = jnp.dot(routed_x, expert_in, preferred_element_type=jnp.float32)
    tanh_part = jnp.tanh(GELU_SCALE * (hidden_pre + GELU_CUBIC * hidden_pre * hidden_pre * hidden_pre))
    activated = (0.5 * hidden_pre * (1.0 + tanh_part)).astype(jnp.bfloat16)
    upstream = jnp.dot(routed_dy, expert_out.T, preferred_element_type=jnp.float32)
    gate_part = jnp.sum(activated.astype(jnp.float32) * upstream, axis=1)
    slope = 0.5 * (1.0 + tanh_part) + 0.5 * hidden_pre * (1.0 - tanh_part * tanh_part) * GELU_SCALE * (1.0 + 3.0 * GELU_CUBIC * hidden_pre * hidden_pre)
    gate_col = routed_gate.astype(jnp.float32)[:, None]
    grad_hidden = (gate_col * upstream * slope).astype(jnp.bfloat16)
    scaled_dy = (gate_col * routed_dy.astype(jnp.float32)).astype(jnp.bfloat16)
    grad_in = jnp.dot(routed_x.T, grad_hidden, preferred_element_type=jnp.float32)
    grad_out_w = jnp.dot(activated.T, scaled_dy, preferred_element_type=jnp.float32)
    hidden_blocks = grad_hidden.astype(jnp.float32).reshape(-1, N_DP, FF // N_DP)
    weight_blocks = expert_in.astype(jnp.float32).reshape(D, N_DP, FF // N_DP)
    partial_sums = jnp.einsum('rbf,dbf->rbd', hidden_blocks, weight_blocks)
    rounded = lax.optimization_barrier(partial_sums.astype(jnp.bfloat16)).astype(jnp.float32)
    return jnp.sum(rounded, axis=1), gate_part, grad_in, grad_out_w


def pick_rows(table, slot_index):
    return table[slot_index]


def reference(tokens, grad_out, expert_ids, gate_values, weight_in, weight_out):
    slot_x, slot_dy, slot_gate, slot_index = jax.vmap(dispatch_one)(
        tokens.reshape(DEVICES, TOK_DEV, D),
        grad_out.reshape(DEVICES, TOK_DEV, D),
        gate_values.reshape(DEVICES, TOK_DEV, TOP),
        expert_ids.reshape(DEVICES, TOK_DEV, TOP))
    slot_dx, slot_gpart, grad_weight_in, grad_weight_out = lax.map(
        expert_grads, (by_expert(slot_x), by_expert(slot_dy), by_expert(slot_gate), weight_in, weight_out))
    back_dx = by_device(slot_dx)
    back_gate = by_device(slot_gpart)
    picked_dx = jax.vmap(pick_rows)(back_dx, slot_index)
    grad_tokens = jnp.sum(picked_dx.reshape(DEVICES, TOK_DEV, TOP, D), axis=2).reshape(TOKENS, D).astype(jnp.bfloat16)
    grad_gates = jax.vmap(pick_rows)(back_gate, slot_index).reshape(TOKENS, TOP)
    return grad_tokens, grad_gates, grad_weight_in, grad_weight_out
```

```python
import functools

import jax
import jax.numpy as jnp
from jax import lax
from jax.experimental import pallas as pl
from jax.experimental.pallas import tpu as pltpu
from jax.sharding import PartitionSpec as P

MESH = pl.DeviceIdType.MESH
BF, F32 = jnp.bfloat16, jnp.float32
GELU_SCALE = 0.7978845608028654
GELU_CUBIC = 0.044715

D = 1024
HID = 256
TOK = 128
CAP = 10
ROWS = 8 * CAP
RET = 48

PLACE = {0: 0, 1: 1, 7: 2, 2: 3, 6: 4, 3: 5, 5: 6, 4: 7}
ORDER = (1, 7, 2, 6, 3, 5, 4)


def dot(a, b):
    return lax.dot_general(a, b, (((1,), (0,)), ((), ())), preferred_element_type=F32)


def dot_nt(a, b):
    return lax.dot_general(a, b, (((1,), (1,)), ((), ())), preferred_element_type=F32)


def dot_tn(a, b):
    return lax.dot_general(a, b, (((0,), (0,)), ((), ())), preferred_element_type=F32)


def iota(shape, dim):
    return lax.broadcasted_iota(jnp.int32, shape, dim)


def kernel(
    tok, gout, meta, win, wout,
    gtok_o, ggate_o, gwin_o, gwout_o,
    raw, meta_far, ms, mr, xs, ds, xo, do,
    wi, wo, act, dpre, dtacc, gacc, dt, rb, gp, gr,
    dwi, dwo, yri, yro, fin_li, fin_lo, fin_ri, fin_ro,
    pack, rets, retr,
    core_s, core_r, loc_s, xs_s, xs_r, zx_s, zx_r, zf_s, zo_s, ya_s, ya_r,
    zb_s, zb_r, gt_s, gt_r, yb_s, yb_r, rt_s, rt_r,
):
    dp, ex = lax.axis_index("dp"), lax.axis_index("expert")
    zl, y = dp // 4, dp % 4
    zh, x, c = ex // 8, (ex // 2) % 4, ex % 2
    z = zh * 4 + zl

    def dev(dz=0, dy=0, dx=0, dc=0):
        zz, yy, xx, cc = (z + dz + 8) % 8, (y + dy + 4) % 4, (x + dx + 4) % 4, (c + dc) % 2
        return ((zz % 4) * 4 + yy, (zz // 4) * 8 + xx * 2 + cc)

    def remote(src, dst, send, recv, to):
        return pltpu.make_async_remote_copy(
            src_ref=src, dst_ref=dst, send_sem=send, recv_sem=recv, device_id=to, device_id_type=MESH
        )

    barrier = pltpu.get_barrier_semaphore()
    partners = [dev(dz=k) for k in range(1, 8)] + [dev(dy=1), dev(dy=3)]
    partners += [dev(dx=k, dc=j) for k in range(4) for j in range(2) if k or j]
    for to in partners:
        pl.semaphore_signal(barrier, inc=1, device_id=to, device_id_type=MESH)
    pl.semaphore_wait(barrier, len(partners))

    sent = []

    def start(copy):
        copy.start()
        sent.append(copy)
        return copy

    right, left = dev(dy=1), dev(dy=3)

    def y_gather(e, kind):
        src = {
            "i_r": (win.at[e], wi.at[e, 3], right, 0),
            "o_r": (wout.at[e], wo.at[e, 3], right, 1),
            "i_l": (win.at[e], wi.at[e, 1], left, 2),
            "o_l": (wout.at[e], wo.at[e, 1], left, 3),
            "i_f": (wi.at[e, 3], wi.at[e, 2], right, 4),
            "o_f": (wo.at[e, 1], wo.at[e, 2], left, 5),
        }[kind]
        return remote(src[0], src[1], ya_s.at[e, src[3]], ya_r.at[e, src[3]], src[2])

    def y_own(e):
        for kind in ("i_r", "o_l", "o_r", "i_l"):
            start(y_gather(e, kind))

    def y_forward(e):
        y_gather(e, "i_r").wait_recv()
        start(y_gather(e, "i_f"))
        y_gather(e, "o_l").wait_recv()
        start(y_gather(e, "o_f"))

    def y_rest(e):
        for kind in ("o_r", "i_l", "i_f", "o_f"):
            y_gather(e, kind).wait_recv()

    y_own(0)
    core = dev(dc=1)
    swaps = [
        remote(meta, meta_far, core_s.at[0], core_r.at[0], core),
        remote(tok, raw.at[pl.ds(TOK, TOK)], core_s.at[1], core_r.at[1], core),
        remote(gout, raw.at[pl.ds(3 * TOK, TOK)], core_s.at[2], core_r.at[2], core),
    ]
    for copy in swaps:
        start(copy)
    local = []
    for e in range(2):
        local.append(pltpu.make_async_copy(win.at[e], wi.at[e, 0], loc_s.at[e, 0]))
        local.append(pltpu.make_async_copy(wout.at[e], wo.at[e, 0], loc_s.at[e, 1]))
    for copy in local:
        copy.start()

    raw[0:TOK, :] = tok[...]
    raw[2 * TOK : 3 * TOK, :] = gout[...]
    gp[...] = jnp.zeros_like(gp)
    before = (iota((TOK, TOK), 0) < iota((TOK, TOK), 1)).astype(F32).astype(BF)

    def ranks(ids0, ids1, wanted):
        hit0, hit1 = ids0 == wanted, ids1 == wanted
        hit = jnp.where(hit0 | hit1, 1.0, 0.0)
        return hit, dot(hit.astype(BF), before), hit0, hit1

    number = iota((32, TOK), 0)
    own0, own1 = meta[0:1, :], meta[1:2, :]
    _, own_rank, hit0, hit1 = ranks(own0, own1, number.astype(F32))
    num_ex = number >> 1
    xr = (((num_ex >> 1) & 3) - x + 4) & 3
    cr = (num_ex + c) & 1
    zr = ((num_ex >> 3) + zh) & 1
    message = (xr * 2 + cr) * RET
    row_code = (message + zr * 20 + (number & 1) * 10).astype(F32) + own_rank
    gate_code = (message + 40 + zr * 2 + (number & 1)).astype(F32)
    lane_code = (((4 - xr) & 3) * 20 + cr * 10).astype(F32) + own_rank

    def pick(hit, table):
        return jnp.sum(jnp.where(hit, table, 0.0), axis=0, keepdims=True).astype(jnp.int32)

    home = [[pick(hit, t) for t in (row_code, gate_code, lane_code)] for hit in (hit0, hit1)]

    for copy in swaps:
        copy.wait_recv()

    k = iota((16, TOK), 0)
    k_x, k_zone, k_e = (x + ((k >> 1) & 3)) & 3, (zh + (k & 1)) & 1, k >> 3
    wanted = ((k_zone * 8 + k_x * 2 + c) * 2 + k_e).astype(F32)
    codes, gates = [], []
    for side, m in enumerate((meta, meta_far)):
        hit, rank, h0, h1 = ranks(m[0:1, :], m[1:2, :], wanted)
        codes.append(jnp.where(hit > 0.0, rank + side * CAP, -1.0))
        gates.append(jnp.where(h0, m[2:3, :], 0.0) + jnp.where(h1, m[3:4, :], 0.0))
    far = [jnp.where(v >= 0.0, v + 20.0, -1.0) for v in codes]
    code = jnp.concatenate(codes + far, axis=1).astype(jnp.int32)
    weight = jnp.concatenate([jnp.ones((16, 2 * TOK), F32)] + gates, axis=1)

    def x_send(e, k):
        return remote(
            ms.at[e, pl.ds(k * 80, 80)], mr.at[e, pl.ds((4 - k) % 4 * 80, 80)],
            xs_s.at[e, k], xs_r.at[e, k], dev(dx=k),
        )

    def dispatch(e):
        blocks = []
        for k in range(8):
            at = e * 8 + k
            same = iota((40, 4 * TOK), 0) == code[at : at + 1, :]
            blocks.append(jnp.where(same, weight[at : at + 1, :], 0.0))
        spread = jnp.concatenate(blocks, axis=0).astype(BF)
        rows = dot(spread, raw[...]).astype(BF)
        ms[e] = rows
        for k in (1, 3, 2):
            start(x_send(e, k))
        mr[e, 0:80, :] = rows[0:80, :]

    dispatch(0)
    dispatch(1)

    o, i = iota((320, 320), 0), iota((320, 320), 1)
    oa, ia = o // 20, i // 20
    unpack = ((o - oa * 20 == i - ia * 20) & ((oa & 3) == (ia >> 2)) & ((oa >> 2) == (ia & 3)))
    unpack = unpack.astype(F32).astype(BF)

    def arrive(e):
        for k in (1, 3, 2):
            x_send(e, k).wait_recv()
        rows = dot(unpack, mr[e]).astype(BF)
        xs[e, 0:80, :] = rows[0:80, :]
        ds[e, 0:80, :] = rows[80:160, :]
        xo[e] = rows[160:240, :]
        do[e] = rows[240:320, :]

    def place(at):
        return pl.ds(at * ROWS, ROWS)

    def z_copy(e, part, src, at, to, send):
        where = (xs, ds)[part]
        return remote(src, where.at[e, place(at)], send, zx_r.at[e, part, at], to)

    cond_sent = []

    def z_own(e):
        for part in range(2):
            mine = (xs, ds)[part].at[e, place(0)]

            def go(way, rho, dz):
                return z_copy(e, part, mine, PLACE[rho], dev(dz=dz), zx_s.at[e, part, way])

            to_right, to_left = go(0, 7, 1), go(1, 1, 7)
            cond_sent.append((zl < 3, to_right))
            cond_sent.append((zl > 0, to_left))
            pl.when(zl < 3)(to_right.start)
            pl.when(zl > 0)(to_left.start)
        for part in range(2):
            theirs = (xo, do)[part].at[e]
            at = jnp.where(zl == 0, PLACE[1], jnp.where(zl == 1, PLACE[2], jnp.where(zl == 2, PLACE[6], PLACE[7])))
            hop = jnp.where(zl < 2, 7 - zl, 4 - zl)
            start(z_copy(e, part, theirs, at, dev(dz=hop), zo_s.at[e, part]))

    def is_right(rho):
        return zl >= 6 - rho

    def z_pass(e, rho):
        at = PLACE[rho]
        goes_right = is_right(rho)
        forward = jnp.where(goes_right, zl < 3, zl > 0)
        there = jnp.where(goes_right, PLACE[rho - 1], PLACE[(rho + 1) % 8])
        to = dev(dz=jnp.where(goes_right, 1, 7))
        for part in range(2):
            here = (xs, ds)[part].at[e, place(at)]
            z_copy(e, part, here, at, to, zf_s.at[e, part, at]).wait_recv()
            on = z_copy(e, part, here, there, to, zf_s.at[e, part, at])
            cond_sent.append((forward, on))
            pl.when(forward)(on.start)

    ones = jnp.ones((8, HID), F32)

    def compute(e, g):
        at = pl.ds(g * 2 * ROWS, 2 * ROWS)
        dtacc[...] = jnp.zeros_like(dtacc)
        gacc[...] = jnp.zeros_like(gacc)

        def shard(j, _):
            w_in = wi[e, j]
            pre = dot(xs[e, at, :], w_in)
            up = dot_nt(ds[e, at, :], wo[e, j])
            sq = pre * pre
            s = jnp.tanh(GELU_SCALE * (pre + GELU_CUBIC * sq * pre))
            half = 0.5 * (1.0 + s)
            a = (pre * half).astype(BF)
            slope = half + 0.5 * pre * (1.0 - s * s) * GELU_SCALE * (1.0 + 3.0 * GELU_CUBIC * sq)
            d = (up * slope).astype(BF)
            act[j, at, :] = a
            dpre[j, at, :] = d
            gacc[...] += a.astype(F32) * up
            dtacc[...] += dot_nt(d, w_in)
            return 0

        lax.fori_loop(0, 4, shard, 0)
        dt[e, at, :] = dtacc[...].astype(BF)
        for k in range(2):
            sums = lax.dot_general(
                ones, gacc[k * ROWS : (k + 1) * ROWS, :], (((1,), (1,)), ((), ())),
                precision=lax.Precision.HIGHEST, preferred_element_type=F32,
            )
            gp[2 * g + k, e * 8 : e * 8 + 8, 0:ROWS] = sums

    def y_scatter(e, kind):
        src = {
            "i_2": (dwi.at[e, 2], yri.at[e], right, 0),
            "o_2": (dwo.at[e, 2], yro.at[e], left, 1),
            "o_1": (dwo.at[e, 1], fin_lo.at[e], right, 2),
            "i_3": (dwi.at[e, 3], fin_ri.at[e], left, 3),
            "i_1": (dwi.at[e, 1], fin_li.at[e], right, 4),
            "o_3": (dwo.at[e, 3], fin_ro.at[e], left, 5),
        }[kind]
        return remote(src[0], src[1], yb_s.at[e, src[3]], yb_r.at[e, src[3]], src[2])

    def weight_grads(e):
        def part_in(j):
            return lambda t: dot_tn(xs[e, :, pl.ds(pl.multiple_of(t * 256, 256), 256)], dpre[j])

        def part_out(j):
            return lambda t: dot_tn(act[j], ds[e, :, pl.ds(pl.multiple_of(t * 256, 256), 256)])

        for j in (2, 1, 3, 0):

            def tile(t, _):
                cols = pl.ds(pl.multiple_of(t * 256, 256), 256)
                g_in, g_out = part_in(j)(t), part_out(j)(t)
                if j:
                    dwi[e, j, cols, :] = g_in.astype(BF)
                    dwo[e, j, :, cols] = g_out.astype(BF)
                else:
                    gwin_o[e, cols, :] = g_in
                    gwout_o[e, :, cols] = g_out
                return 0

            lax.fori_loop(0, 4, tile, 0)
            for kind in {2: ("i_2", "o_2"), 1: ("o_1",), 3: ("i_3",), 0: ()}[j]:
                start(y_scatter(e, kind))

    def y_relay(e):
        y_scatter(e, "i_2").wait_recv()
        dwi[e, 1] = (dwi[e, 1].astype(F32) + yri[e].astype(F32)).astype(BF)
        start(y_scatter(e, "i_1"))
        y_scatter(e, "o_2").wait_recv()
        dwo[e, 3] = (dwo[e, 3].astype(F32) + yro[e].astype(F32)).astype(BF)
        start(y_scatter(e, "o_3"))

    def y_final(e):
        for kind in ("o_1", "i_3", "i_1", "o_3"):
            y_scatter(e, kind).wait_recv()
        gwin_o[e] = gwin_o[e] + fin_li[e].astype(F32) + fin_ri[e].astype(F32)
        gwout_o[e] = gwout_o[e] + fin_lo[e].astype(F32) + fin_ro[e].astype(F32)

    def z_back(e, rho):
        at = place(PLACE[rho])
        goes_right = is_right(rho)
        incoming = jnp.where(goes_right, zl < 3, zl > 0)
        first = jnp.where(goes_right, zl == 0, zl == 3)
        slot = jnp.where(first, 9, jnp.where(goes_right, rho + 1, rho - 1))
        hop = jnp.where(first, rho, jnp.where(goes_right, 7, 1))
        here = dt.at[e, at]

        @pl.when(incoming)
        def _():
            remote(here, rb.at[e, rho], zb_s.at[e, rho], zb_r.at[e, rho], dev(dz=1)).wait_recv()
            dt[e, at, :] = (dt[e, at, :].astype(F32) + rb[e, rho].astype(F32)).astype(BF)

        start(remote(here, rb.at[e, slot], zb_s.at[e, rho], zb_r.at[e, slot], dev(dz=hop)))

    def z_home(e):
        total = dt[e, 0:ROWS, :].astype(F32)
        dtacc[0:ROWS, :] = total
        here = dt.at[e, place(0)]
        for cond, slot in ((zl < 3, 8), (zl > 0, 0)):

            @pl.when(cond)
            def _(slot=slot):
                remote(here, rb.at[e, slot], zb_s.at[e, 0], zb_r.at[e, slot], dev(dz=1)).wait_recv()
                dtacc[0:ROWS, :] += rb[e, slot].astype(F32)

        pack[e * ROWS : (e + 1) * ROWS, :] = dtacc[0:ROWS, :].astype(BF)
        remote(here, rb.at[e, 9], zb_s.at[e, 0], zb_r.at[e, 9], dev(dz=1)).wait_recv()
        pack[(2 + e) * ROWS : (3 + e) * ROWS, :] = rb[e, 9]

    def gate_copy(rho):
        return remote(gp.at[PLACE[rho]], gr.at[8 - rho], gt_s.at[rho], gt_r.at[8 - rho], dev(dz=rho))

    def back(rhos, e):
        for rho in rhos:
            z_back(e, rho)

    def z_passes(e, rhos):
        for rho in rhos:
            z_pass(e, rho)

    arrive(0)
    z_own(0)
    y_forward(0)
    y_own(1)
    z_passes(0, (1, 7))
    arrive(1)
    z_passes(0, (2, 6))
    for copy in local:
        copy.wait()
    y_rest(0)
    compute(0, 0)
    z_passes(0, (3, 5, 4))
    z_own(1)
    compute(0, 1)
    y_forward(1)
    compute(0, 2)
    compute(0, 3)
    z_passes(1, (1, 7))
    weight_grads(0)
    back((4, 5, 3), 0)
    z_passes(1, (2, 6))
    back((6, 2), 0)
    y_rest(1)
    compute(1, 0)
    y_relay(0)
    z_passes(1, (3, 5, 4))
    compute(1, 1)
    back((7, 1), 0)
    compute(1, 2)
    compute(1, 3)
    for rho in ORDER:
        start(gate_copy(rho))
    back((4, 5, 3), 1)
    weight_grads(1)
    z_home(0)
    back((6, 2, 7, 1), 1)
    y_final(0)
    z_home(1)

    own_sum, other_sum = gp[0], jnp.zeros((16, 128), F32)
    for rho in range(1, 8):
        gate_copy(8 - rho).wait_recv()
        near = jnp.where(rho < 4, rho <= 3 - zl, rho >= 8 - zl)
        value = gr[rho]
        own_sum += jnp.where(near, value, 0.0)
        other_sum += jnp.where(near, 0.0, value)
    line = iota((16, 128), 0)
    rows = jnp.zeros((16, 128), F32)
    for at, value in enumerate((own_sum[0:1], own_sum[8:9], other_sum[0:1], other_sum[8:9])):
        high = value.astype(BF).astype(F32)
        rows = jnp.where(line == at, high, jnp.where(line == at + 4, value - high, rows))
    pack[320:336, :] = jnp.zeros((16, D), BF)
    pack[320:336, 0:128] = rows.astype(BF)

    o, i = iota((8 * RET, 336), 0), iota((8 * RET, 336), 1)
    m, w = o // RET, o - (o // RET) * RET
    q = w // 10
    source = jnp.where(w < 40, q * ROWS + m * 10 + (w - q * 10), 320 + w - 40)
    chosen = (source == i).astype(F32).astype(BF)
    rets[...] = dot(chosen, pack[...]).astype(BF)

    def ret_copy(k, j):
        m = k * 2 + j
        n = (4 - k) % 4 * 2 + j
        return remote(
            rets.at[pl.ds(m * RET, RET)], retr.at[pl.ds(n * RET, RET)], rt_s.at[m], rt_r.at[n], dev(dx=k, dc=j)
        )

    peers = [(k, j) for k in (2, 1, 3, 0) for j in range(2) if k or j]
    for k, j in peers:
        start(ret_copy(k, j))
    retr[0:RET, :] = rets[0:RET, :]
    y_relay(1)
    for k, j in peers:
        ret_copy(k, j).wait_recv()
    line = iota((8 * RET, TOK), 0)
    both = (line == home[0][0]) | (line == home[1][0])
    gtok_o[...] = dot_tn(both.astype(F32).astype(BF), retr[...]).astype(BF)
    for k in range(2):
        gate_row, lane = home[k][1], home[k][2]
        rows_of = ((line == gate_row) | (line == gate_row + 4)).astype(F32).astype(BF)
        found = dot_tn(retr[:, 0:128], rows_of)
        value = jnp.sum(jnp.where(iota((128, TOK), 0) == lane, found, 0.0), axis=0, keepdims=True)
        ggate_o[k : k + 1, :] = value / meta[2 + k : 3 + k, :]
    y_final(1)
    for copy in sent:
        copy.wait_send()
    for cond, copy in cond_sent:
        pl.when(cond)(copy.wait_send)


def per_device(tokens, grad_out, expert_ids, gate_values, weight_in, weight_out):
    ids, gates = expert_ids.T.astype(F32), gate_values.T.astype(F32)
    meta = jnp.concatenate([ids, gates, jnp.zeros((4, TOK), F32)], axis=0)
    v, dma = pltpu.VMEM, pltpu.SemaphoreType.DMA
    scratch = [
        v((4 * TOK, D), BF), v((8, TOK), F32), v((2, 320, D), BF), v((2, 320, D), BF),
        v((2, 640, D), BF), v((2, 640, D), BF), v((2, ROWS, D), BF), v((2, ROWS, D), BF),
        v((2, 4, D, HID), BF), v((2, 4, HID, D), BF), v((4, 640, HID), BF), v((4, 640, HID), BF),
        v((2 * ROWS, D), F32), v((2 * ROWS, HID), F32), v((2, 640, D), BF), v((2, 10, ROWS, D), BF),
        v((8, 16, 128), F32), v((8, 16, 128), F32),
        v((2, 4, D, HID), BF), v((2, 4, HID, D), BF), v((2, D, HID), BF), v((2, HID, D), BF),
        v((2, D, HID), BF), v((2, HID, D), BF), v((2, D, HID), BF), v((2, HID, D), BF),
        v((336, D), BF), v((8 * RET, D), BF), v((8 * RET, D), BF),
        dma((3,)), dma((3,)), dma((2, 2)), dma((2, 4)), dma((2, 4)),
        dma((2, 2, 2)), dma((2, 2, 8)), dma((2, 2, 8)), dma((2, 2)), dma((2, 6)), dma((2, 6)),
        dma((2, 8)), dma((2, 10)), dma((8,)), dma((8,)), dma((2, 6)), dma((2, 6)), dma((8,)), dma((8,)),
    ]
    vm, hbm = pl.BlockSpec(memory_space=pltpu.VMEM), pl.BlockSpec(memory_space=pl.ANY)
    gtok, ggate, gwin, gwout = pl.pallas_call(
        kernel,
        out_shape=[
            jax.ShapeDtypeStruct((TOK, D), BF),
            jax.ShapeDtypeStruct((2, TOK), F32),
            jax.ShapeDtypeStruct((2, D, HID), F32),
            jax.ShapeDtypeStruct((2, HID, D), F32),
        ],
        in_specs=[vm, vm, vm, hbm, hbm],
        out_specs=[vm, vm, vm, vm],
        scratch_shapes=scratch,
        compiler_params=pltpu.CompilerParams(
            collective_id=0, has_side_effects=True, vmem_limit_bytes=62 * 2**20
        ),
        name="moe_backward",
    )(tokens, grad_out, meta, weight_in, weight_out)
    return gtok, ggate.T, gwin, gwout


def solution(mesh):
    placed = (
        P(("dp", "expert"), None),
        P(("dp", "expert"), None),
        P(("dp", "expert"), None),
        P(("dp", "expert"), None),
        P("expert", None, "dp"),
        P("expert", "dp", None),
    )
    return jax.shard_map(
        per_device,
        mesh=mesh,
        in_specs=placed,
        out_specs=(
            P(("dp", "expert"), None),
            P(("dp", "expert"), None),
            P("expert", None, "dp"),
            P("expert", "dp", None),
        ),
        check_vma=False,
    )
```

```python
import functools

import jax
import jax.numpy as jnp
from jax import lax
from jax.experimental import pallas as pl
from jax.experimental.pallas import tpu as pltpu
from jax.sharding import PartitionSpec as P

MESH = pl.DeviceIdType.MESH
BF, F32 = jnp.bfloat16, jnp.float32
GELU_SCALE = 0.7978845608028654
GELU_CUBIC = 0.044715

D = 1024
HID = 256
TOK = 128
CAP = 10
ROWS = 8 * CAP
RET = 32

PLACE = {7: 0, 1: 1, 6: 2, 2: 3, 5: 4, 3: 5, 4: 6, 0: 7}
OWN = slice(PLACE[0] * ROWS, PLACE[0] * ROWS + ROWS)
ORDER = (1, 7, 2, 6, 3, 5, 4)


def dot(a, b):
    return lax.dot_general(a, b, (((1,), (0,)), ((), ())), preferred_element_type=F32)


def dot_nt(a, b):
    return lax.dot_general(a, b, (((1,), (1,)), ((), ())), preferred_element_type=F32)


def dot_tn(a, b):
    return lax.dot_general(a, b, (((0,), (0,)), ((), ())), preferred_element_type=F32)


def iota(shape, dim):
    return lax.broadcasted_iota(jnp.int32, shape, dim)


def kernel(
    tok, gout, ids, gate, win, wout,
    gtok_o, ggate_o, own_io, own_oo, fin_li, fin_lo, fin_ri, fin_ro,
    raw, meta, meta_far, ms, mr, xs, ds, xo, do,
    wi, wo, act, dpre, dtacc, gacc, dt, rb, gp, gr,
    dwi, dwo, yri, yro, own_i, own_o,
    pack, rets, retr,
    core_s, core_r, loc_s, xs_s, xs_r, zx_s, zx_r, zf_s, zo_s, ya_s, ya_r,
    zb_s, zb_r, gt_s, gt_r, yb_s, yb_r, rt_s, rt_r, out_s,
):
    dp, ex = lax.axis_index("dp"), lax.axis_index("expert")
    zl, y = dp // 4, dp % 4
    zh, x, c = ex // 8, (ex // 2) % 4, ex % 2
    z = zh * 4 + zl

    def dev(dz=0, dy=0, dx=0, dc=0):
        zz, yy, xx, cc = (z + dz + 8) % 8, (y + dy + 4) % 4, (x + dx + 4) % 4, (c + dc) % 2
        return ((zz % 4) * 4 + yy, (zz // 4) * 8 + xx * 2 + cc)

    def remote(src, dst, send, recv, to):
        return pltpu.make_async_remote_copy(
            src_ref=src, dst_ref=dst, send_sem=send, recv_sem=recv, device_id=to, device_id_type=MESH
        )

    barrier = pltpu.get_barrier_semaphore()
    partners = [dev(dz=k) for k in range(1, 8)] + [dev(dy=1), dev(dy=3)]
    partners += [dev(dx=k, dc=j) for k in range(4) for j in range(2) if k or j]
    for to in partners:
        pl.semaphore_signal(barrier, inc=1, device_id=to, device_id_type=MESH)
    pl.semaphore_wait(barrier, len(partners))

    sent = []

    def start(copy):
        copy.start()
        sent.append(copy)
        return copy

    right, left = dev(dy=1), dev(dy=3)

    def y_gather(e, kind):
        src = {
            "i_r": (win.at[e], wi.at[e, 3], right, 0),
            "o_r": (wout.at[e], wo.at[e, 3], right, 1),
            "i_l": (win.at[e], wi.at[e, 1], left, 2),
            "o_l": (wout.at[e], wo.at[e, 1], left, 3),
            "i_f": (wi.at[e, 3], wi.at[e, 2], right, 4),
            "o_f": (wo.at[e, 1], wo.at[e, 2], left, 5),
        }[kind]
        return remote(src[0], src[1], ya_s.at[e, src[3]], ya_r.at[e, src[3]], src[2])

    def y_own(e, kinds):
        for kind in kinds:
            start(y_gather(e, kind))

    def y_forward(e):
        y_gather(e, "i_r").wait_recv()
        start(y_gather(e, "i_f"))
        y_gather(e, "o_l").wait_recv()
        start(y_gather(e, "o_f"))

    def y_rest(e):
        for kind in ("o_r", "i_l", "i_f", "o_f"):
            y_gather(e, kind).wait_recv()

    meta[...] = jnp.concatenate([ids[...].astype(F32), gate[...].astype(F32), jnp.zeros((4, TOK), F32)], axis=0)
    core = dev(dc=1)
    swaps = [
        remote(meta, meta_far, core_s.at[0], core_r.at[0], core),
        remote(tok, raw.at[pl.ds(TOK, TOK)], core_s.at[1], core_r.at[1], core),
        remote(gout, raw.at[pl.ds(3 * TOK, TOK)], core_s.at[2], core_r.at[2], core),
    ]
    for copy in swaps:
        start(copy)
    y_own(0, ("i_r", "o_l"))
    local = []
    for e in range(2):
        local.append(pltpu.make_async_copy(win.at[e], wi.at[e, 0], loc_s.at[e, 0]))
        local.append(pltpu.make_async_copy(wout.at[e], wo.at[e, 0], loc_s.at[e, 1]))
    for copy in local:
        copy.start()

    raw[0:TOK, :] = tok[...]
    raw[2 * TOK : 3 * TOK, :] = gout[...]
    before = (iota((TOK, TOK), 0) < iota((TOK, TOK), 1)).astype(F32).astype(BF)

    def ranks(ids0, ids1, wanted):
        hit0, hit1 = ids0 == wanted, ids1 == wanted
        hit = jnp.where(hit0 | hit1, 1.0, 0.0)
        return hit, dot(hit.astype(BF), before), hit0, hit1

    swaps[0].wait_recv()
    k = iota((16, TOK), 0)
    k_x, k_zone, k_e = (x + (k >> 2)) & 3, (zh + (k & 1)) & 1, (k >> 1) & 1
    wanted = ((k_zone * 8 + k_x * 2 + c) * 2 + k_e).astype(F32)
    codes, gates = [], []
    for side, m in enumerate((meta, meta_far)):
        hit, rank, h0, h1 = ranks(m[0:1, :], m[1:2, :], wanted)
        codes.append(jnp.where(hit > 0.0, rank + side * CAP, -1.0))
        gates.append(jnp.where(h0, m[2:3, :], 0.0) + jnp.where(h1, m[3:4, :], 0.0))
    code = jnp.concatenate(codes, axis=1).astype(jnp.int32)
    weight = jnp.concatenate(gates, axis=1)

    def x_send(part, k):
        return remote(
            ms.at[part, pl.ds(k * 80, 80)], mr.at[part, pl.ds((4 - k) % 4 * 80, 80)],
            xs_s.at[part, k], xs_r.at[part, k], dev(dx=k),
        )

    def dispatch(part):
        blocks = []
        for k in range(16):
            same = iota((20, 2 * TOK), 0) == code[k : k + 1, :]
            blocks.append(jnp.where(same, weight[k : k + 1, :] if part else 1.0, 0.0))
        spread = jnp.concatenate(blocks, axis=0).astype(BF)
        rows = dot(spread, raw[part * 2 * TOK : (part + 1) * 2 * TOK, :]).astype(BF)
        ms[part] = rows
        for k in (1, 3, 2):
            start(x_send(part, k))
        mr[part, 0:80, :] = rows[0:80, :]

    swaps[1].wait_recv()
    dispatch(0)
    swaps[2].wait_recv()
    dispatch(1)
    y_own(0, ("o_r", "i_l"))
    gp[...] = jnp.zeros_like(gp)

    number = iota((32, TOK), 0)
    own0, own1 = meta[0:1, :], meta[1:2, :]
    _, own_rank, hit0, hit1 = ranks(own0, own1, number.astype(F32))
    num_ex = number >> 1
    xr = (((num_ex >> 1) & 3) - x + 4) & 3
    cr = (num_ex + c) & 1
    zr = ((num_ex >> 3) + zh) & 1
    message = (number & 1) * (8 * RET) + (xr * 2 + cr) * RET
    row_code = (message + zr * 10).astype(F32) + own_rank
    gate_code = (message + 20 + zr).astype(F32)
    lane_code = (((4 - xr) & 3) * 20 + cr * 10).astype(F32) + own_rank

    def pick(hit, table):
        return jnp.sum(jnp.where(hit, table, 0.0), axis=0, keepdims=True).astype(jnp.int32)

    home = [[pick(hit, t) for t in (row_code, gate_code, lane_code)] for hit in (hit0, hit1)]

    o, i = iota((320, 320), 0), iota((320, 320), 1)
    oa, ia = o // 20, i // 20
    unpack = ((o - oa * 20 == i - ia * 20) & ((oa & 3) == (ia >> 2)) & ((oa >> 2) == (ia & 3)))
    unpack = unpack.astype(F32).astype(BF)

    def arrive(part):
        for k in (1, 3, 2):
            x_send(part, k).wait_recv()
        rows = dot(unpack, mr[part]).astype(BF)
        mine, theirs = (xs, ds)[part], (xo, do)[part]
        for e in range(2):
            mine[e, OWN, :] = rows[e * 160 : e * 160 + 80, :]
            theirs[e] = rows[e * 160 + 80 : e * 160 + 160, :]

    def place(at):
        return pl.ds(at * ROWS, ROWS)

    def z_copy(e, part, src, at, to, send):
        where = (xs, ds)[part]
        return remote(src, where.at[e, place(at)], send, zx_r.at[e, part, at], to)

    cond_sent = []

    def z_own(e, busy, parts=(0, 1)):
        def send(cond, copy):
            cond_sent.append((cond, copy))
            pl.when(cond)(copy.start)

        for part in parts:
            mine, theirs = (xs, ds)[part].at[e, place(PLACE[0])], (xo, do)[part].at[e]

            def go(way, rho, dz):
                return z_copy(e, part, mine, PLACE[rho], dev(dz=dz), zx_s.at[e, part, way])

            inner = (zl == 1) | (zl == 2)
            at = jnp.where(zl == 0, PLACE[1], jnp.where(zl == 1, PLACE[2], jnp.where(zl == 2, PLACE[6], PLACE[7])))
            hop = jnp.where(zl < 2, 7 - zl, 4 - zl)
            send(zl == 2 if busy else zl < 2, go(0, 7, 1))
            send(zl == 1 if busy else zl > 1, go(1, 1, 7))
            send(inner if busy else ~inner, z_copy(e, part, theirs, at, dev(dz=hop), zo_s.at[e, part]))

    def is_right(rho):
        return zl >= 6 - rho

    def z_waits(e, rhos, parts=(0, 1)):
        for rho in rhos:
            at = PLACE[rho]
            for part in parts:
                here = (xs, ds)[part].at[e, place(at)]
                z_copy(e, part, here, at, dev(dz=1), zf_s.at[e, part, at]).wait_recv()

    def z_on(e, rho, part):
        at = PLACE[rho]
        goes_right = is_right(rho)
        forward = jnp.where(goes_right, zl < 3, zl > 0)
        there = jnp.where(goes_right, PLACE[rho - 1], PLACE[(rho + 1) % 8])
        to = dev(dz=jnp.where(goes_right, 1, 7))
        return forward, z_copy(e, part, (xs, ds)[part].at[e, place(at)], there, to, zf_s.at[e, part, at])

    def z_passes(e, rhos, parts=(0, 1)):
        for rho in rhos:
            for part in parts:
                z_waits(e, (rho,), (part,))
                forward, on = z_on(e, rho, part)
                pl.when(forward)(on.start)

    ones = jnp.ones((8, HID), F32)

    def compute(e, g):
        at = pl.ds(pl.multiple_of(g * 2 * ROWS, 2 * ROWS), 2 * ROWS)
        dtacc[...] = jnp.zeros_like(dtacc)
        gacc[...] = jnp.zeros_like(gacc)

        def shard(j, _):
            w_in = wi[e, j]
            pre = dot(xs[e, at, :], w_in)
            up = dot_nt(ds[e, at, :], wo[e, j])
            sq = pre * pre
            s = jnp.tanh(GELU_SCALE * (pre + GELU_CUBIC * sq * pre))
            half = 0.5 * (1.0 + s)
            a = (pre * half).astype(BF)
            slope = half + 0.5 * pre * (1.0 - s * s) * GELU_SCALE * (1.0 + 3.0 * GELU_CUBIC * sq)
            d = (up * slope).astype(BF)
            act[j, at, :] = a
            dpre[j, at, :] = d
            gacc[...] += a.astype(F32) * up
            dtacc[...] += dot_nt(d, w_in)
            return 0

        lax.fori_loop(0, 4, shard, 0)
        dt[e, at, :] = dtacc[...].astype(BF)
        for k in range(2):
            sums = lax.dot_general(
                ones, gacc[k * ROWS : (k + 1) * ROWS, :], (((1,), (1,)), ((), ())),
                precision=lax.Precision.HIGHEST, preferred_element_type=F32,
            )
            gp[e, 2 * g + k, :, 0:ROWS] = sums

    def y_scatter(e, kind):
        src = {
            "i_2": (dwi.at[e, 2], yri.at[e], right, 0),
            "o_2": (dwo.at[e, 2], yro.at[e], left, 1),
            "o_1": (dwo.at[e, 1], fin_lo.at[e], right, 2),
            "i_3": (dwi.at[e, 3], fin_ri.at[e], left, 3),
            "i_1": (dwi.at[e, 1], fin_li.at[e], right, 4),
            "o_3": (dwo.at[e, 3], fin_ro.at[e], left, 5),
        }[kind]
        return remote(src[0], src[1], yb_s.at[e, src[3]], yb_r.at[e, src[3]], src[2])

    def weight_grads(e, j):
        def tile(t, _):
            cols = pl.ds(pl.multiple_of(t * 256, 256), 256)
            g_in, g_out = dot_tn(xs[e, :, cols], dpre[j]), dot_tn(act[j], ds[e, :, cols])
            if j:
                dwi[e, j, cols, :] = g_in.astype(BF)
                dwo[e, j, :, cols] = g_out.astype(BF)
            else:
                own_i[e, cols, :] = g_in
                own_o[e, :, cols] = g_out
            return 0

        lax.fori_loop(0, 4, tile, 0)
        for kind in {2: ("i_2", "o_2"), 1: ("o_1",), 3: ("i_3",), 0: ()}[j]:
            start(y_scatter(e, kind))
        if j == 0:
            for k, (a, b) in enumerate(((own_i, own_io), (own_o, own_oo))):
                copy = pltpu.make_async_copy(a.at[e], b.at[e], out_s.at[e, k])
                copy.start()
                outs.append(copy)

    outs = []

    def y_relay(e):
        y_scatter(e, "i_2").wait_recv()
        dwi[e, 1] = (dwi[e, 1].astype(F32) + yri[e].astype(F32)).astype(BF)
        start(y_scatter(e, "i_1"))
        y_scatter(e, "o_2").wait_recv()
        dwo[e, 3] = (dwo[e, 3].astype(F32) + yro[e].astype(F32)).astype(BF)
        start(y_scatter(e, "o_3"))

    def y_final(e):
        for kind in ("o_1", "i_3", "i_1", "o_3"):
            y_scatter(e, kind).wait_recv()

    def z_back(e, rho):
        spot = jnp.where(rho >= 5, 14 - 2 * rho, jnp.where(rho == 4, 6, 2 * rho - 1))
        at = pl.ds(pl.multiple_of(spot * ROWS, ROWS), ROWS)
        goes_right = is_right(rho)
        incoming = jnp.where(goes_right, zl < 3, zl > 0)
        first = jnp.where(goes_right, zl == 0, zl == 3)
        slot = jnp.where(first, 9, jnp.where(goes_right, rho + 1, rho - 1))
        hop = jnp.where(first, rho, jnp.where(goes_right, 7, 1))
        here = dt.at[e, at]

        @pl.when(incoming)
        def _():
            remote(here, rb.at[e, rho], zb_s.at[e, rho], zb_r.at[e, rho], dev(dz=1)).wait_recv()
            dt[e, at, :] = (dt[e, at, :].astype(F32) + rb[e, rho].astype(F32)).astype(BF)

        remote(here, rb.at[e, slot], zb_s.at[e, rho], zb_r.at[e, slot], dev(dz=hop)).start()

    edge = (zl == 0) | (zl == 3)

    def back_edge(e, pairs):
        for at_0, at_3 in pairs:
            pl.when(edge)(lambda: z_back(e, jnp.where(zl == 0, at_0, at_3)))

    def back_inner(e, pairs):
        for at_1, at_2 in pairs:
            pl.when(~edge)(lambda: z_back(e, jnp.where(zl == 1, at_1, at_2)))

    inner_first = ((1, 7), (2, 6), (7, 5), (6, 1))
    inner_last = ((3, 4), (4, 2), (5, 3))
    edge_last = ((7, 1), (6, 2))

    def z_home(e):
        own = dt.at[e, place(PLACE[0])]
        dtacc[0:ROWS, :] = dt[e, OWN, :].astype(F32)
        for cond, slot in ((zl < 3, 8), (zl > 0, 0)):

            @pl.when(cond)
            def _(slot=slot):
                remote(own, rb.at[e, slot], zb_s.at[e, 0], zb_r.at[e, slot], dev(dz=1)).wait_recv()
                dtacc[0:ROWS, :] += rb[e, slot].astype(F32)

        pack[0:ROWS, :] = dtacc[0:ROWS, :].astype(BF)
        remote(own, rb.at[e, 9], zb_s.at[e, 0], zb_r.at[e, 9], dev(dz=1)).wait_recv()
        pack[ROWS : 2 * ROWS, :] = rb[e, 9]

    def gate_copy(e, rho):
        return remote(
            gp.at[e, PLACE[rho]], gr.at[e, 8 - rho], gt_s.at[e, rho], gt_r.at[e, 8 - rho], dev(dz=rho)
        )

    def gates_out(e):
        for rho in ORDER:
            start(gate_copy(e, rho))

    peers = [(k, j) for k in (2, 1, 3, 0) for j in range(2) if k or j]

    def ret_copy(e, k, j):
        m = k * 2 + j
        n = (4 - k) % 4 * 2 + j
        return remote(
            rets.at[e, pl.ds(m * RET, RET)], retr.at[pl.ds(e * 8 * RET + n * RET, RET)],
            rt_s.at[e, m], rt_r.at[e, n], dev(dx=k, dc=j),
        )

    def give_back(e):
        z_home(e)
        own_sum, other_sum = gp[e, PLACE[0]], jnp.zeros((8, 128), F32)
        for rho in range(1, 8):
            gate_copy(e, 8 - rho).wait_recv()
            near = jnp.where(rho < 4, rho <= 3 - zl, rho >= 8 - zl)
            value = gr[e, rho]
            own_sum += jnp.where(near, value, 0.0)
            other_sum += jnp.where(near, 0.0, value)
        line = iota((16, 128), 0)
        rows = jnp.zeros((16, 128), F32)
        for at, value in enumerate((own_sum[0:1], other_sum[0:1])):
            high = value.astype(BF).astype(F32)
            rows = jnp.where(line == at, high, jnp.where(line == at + 2, value - high, rows))
        pack[160:176, :] = jnp.zeros((16, D), BF)
        pack[160:176, 0:128] = rows.astype(BF)
        o, i = iota((8 * RET, 176), 0), iota((8 * RET, 176), 1)
        m, w = o >> 5, o & 31
        q = w // 10
        source = jnp.where(w < 20, q * ROWS + m * 10 + (w - q * 10), 160 + w - 20)
        chosen = (source == i).astype(F32).astype(BF)
        rets[e] = dot(chosen, pack[...]).astype(BF)
        for k, j in peers:
            start(ret_copy(e, k, j))
        retr[e * 8 * RET : e * 8 * RET + RET, :] = rets[e, 0:RET, :]

    def last_passes(e, between):
        if e == 0:
            pl.when(~edge)(lambda: z_passes(e, (3, 5, 4), (1,)))
            z_own(1, True)
        else:
            pl.when(~edge)(lambda: z_passes(e, (3, 5, 4)))
        pl.when(edge)(lambda: z_waits(e, (4,)))
        compute(e, 3)
        back_edge(e, ((4, 4),))
        between()
        pl.when(edge)(lambda: z_waits(e, (3, 5)))
        compute(e, 2)
        back_edge(e, ((3, 5), (5, 3)))

    arrive(0)
    z_own(0, True, (0,))
    z_own(0, False, (0,))
    z_passes(0, (1, 7), (0,))
    arrive(1)
    z_own(0, True, (1,))
    z_own(0, False, (1,))
    y_forward(0)
    z_passes(0, (2, 6), (0,))
    z_passes(0, (1, 7), (1,))
    y_own(1, ("i_r", "o_l"))
    pl.when(~edge)(lambda: z_passes(0, (3, 5, 4), (0,)))
    z_passes(0, (2, 6), (1,))
    z_own(1, False)
    y_own(1, ("o_r", "i_l"))
    for copy in local:
        copy.wait()
    y_rest(0)
    compute(0, 0)
    compute(0, 1)
    back_edge(0, ((1, 7), (2, 6)))
    last_passes(0, lambda: y_forward(1))
    weight_grads(0, 2)
    z_passes(1, (1, 7))
    gates_out(0)
    back_inner(0, inner_first)
    weight_grads(0, 1)
    weight_grads(0, 3)
    z_passes(1, (2, 6))
    weight_grads(0, 0)
    back_inner(0, inner_last)
    back_edge(0, edge_last)
    y_rest(1)
    compute(1, 0)
    y_relay(0)
    compute(1, 1)
    back_edge(1, ((1, 7), (2, 6)))
    last_passes(1, lambda: None)
    weight_grads(1, 2)
    back_inner(1, inner_first)
    gates_out(1)
    give_back(0)
    weight_grads(1, 1)
    weight_grads(1, 3)
    back_inner(1, inner_last)
    back_edge(1, edge_last)
    weight_grads(1, 0)
    y_final(0)
    give_back(1)
    y_relay(1)
    for e in range(2):
        for k, j in peers:
            ret_copy(e, k, j).wait_recv()
    line = iota((16 * RET, TOK), 0)
    both = (line == home[0][0]) | (line == home[1][0])
    gtok_o[...] = dot_tn(both.astype(F32).astype(BF), retr[...]).astype(BF)
    for k in range(2):
        gate_row, lane = home[k][1], home[k][2]
        rows_of = ((line == gate_row) | (line == gate_row + 2)).astype(F32).astype(BF)
        found = dot_tn(retr[:, 0:128], rows_of)
        value = jnp.sum(jnp.where(iota((128, TOK), 0) == lane, found, 0.0), axis=0, keepdims=True)
        ggate_o[k : k + 1, :] = value / meta[2 + k : 3 + k, :]
    y_final(1)
    for copy in sent:
        copy.wait_send()
    cond_sent += [z_on(e, rho, part) for e in range(2) for rho in ORDER for part in range(2)]
    for cond, copy in cond_sent:
        pl.when(cond)(copy.wait_send)
    for e in range(2):
        for rho in range(1, 8):
            remote(dt.at[e, place(0)], rb.at[e, rho], zb_s.at[e, rho], zb_r.at[e, rho], dev(dz=1)).wait_send()
    for copy in outs:
        copy.wait()


def per_device(tokens, grad_out, expert_ids, gate_values, weight_in, weight_out):
    v, dma = pltpu.VMEM, pltpu.SemaphoreType.DMA
    scratch = [
        v((4 * TOK, D), BF), v((8, TOK), F32), v((8, TOK), F32), v((2, 320, D), BF), v((2, 320, D), BF),
        v((2, 640, D), BF), v((2, 640, D), BF), v((2, ROWS, D), BF), v((2, ROWS, D), BF),
        v((2, 4, D, HID), BF), v((2, 4, HID, D), BF), v((4, 640, HID), BF), v((4, 640, HID), BF),
        v((2 * ROWS, D), F32), v((2 * ROWS, HID), F32), v((2, 640, D), BF), v((2, 10, ROWS, D), BF),
        v((2, 8, 8, 128), F32), v((2, 8, 8, 128), F32),
        v((2, 4, D, HID), BF), v((2, 4, HID, D), BF), v((2, D, HID), BF), v((2, HID, D), BF),
        v((2, D, HID), F32), v((2, HID, D), F32),
        v((176, D), BF), v((2, 8 * RET, D), BF), v((16 * RET, D), BF),
        dma((3,)), dma((3,)), dma((2, 2)), dma((2, 4)), dma((2, 4)),
        dma((2, 2, 2)), dma((2, 2, 8)), dma((2, 2, 8)), dma((2, 2)), dma((2, 6)), dma((2, 6)),
        dma((2, 8)), dma((2, 10)), dma((2, 8)), dma((2, 8)), dma((2, 6)), dma((2, 6)), dma((2, 8)), dma((2, 8)),
        dma((2, 2)),
    ]
    vm, hbm = pl.BlockSpec(memory_space=pltpu.VMEM), pl.BlockSpec(memory_space=pl.ANY)
    shapes = [((TOK, D), BF), ((2, TOK), F32), ((2, D, HID), F32), ((2, HID, D), F32)]
    shapes += [((2, D, HID), BF), ((2, HID, D), BF)] * 2
    gtok, ggate, own_i, own_o, left_i, left_o, right_i, right_o = pl.pallas_call(
        kernel,
        out_shape=[jax.ShapeDtypeStruct(*of) for of in shapes],
        in_specs=[vm, vm, vm, vm, hbm, hbm],
        out_specs=[vm, vm, hbm, hbm, hbm, hbm, hbm, hbm],
        scratch_shapes=scratch,
        compiler_params=pltpu.CompilerParams(
            collective_id=0, has_side_effects=True, vmem_limit_bytes=62 * 2**20
        ),
        name="moe_backward",
    )(tokens, grad_out, expert_ids.T, gate_values.T, weight_in, weight_out)
    gwin = own_i + left_i.astype(F32) + right_i.astype(F32)
    gwout = own_o + left_o.astype(F32) + right_o.astype(F32)
    return gtok, ggate.T, gwin, gwout


def solution(mesh):
    placed = (
        P(("dp", "expert"), None),
        P(("dp", "expert"), None),
        P(("dp", "expert"), None),
        P(("dp", "expert"), None),
        P("expert", None, "dp"),
        P("expert", "dp", None),
    )
    return jax.shard_map(
        per_device,
        mesh=mesh,
        in_specs=placed,
        out_specs=(
            P(("dp", "expert"), None),
            P(("dp", "expert"), None),
            P("expert", None, "dp"),
            P("expert", "dp", None),
        ),
        check_vma=False,
    )
```

```python
import functools

import jax
import jax.numpy as jnp
from jax import lax
from jax.experimental import pallas as pl
from jax.experimental.pallas import tpu as pltpu
from jax.sharding import PartitionSpec as P

MESH = pl.DeviceIdType.MESH
BF, F32 = jnp.bfloat16, jnp.float32
GELU_SCALE = 0.7978845608028654
GELU_CUBIC = 0.044715

D = 1024
HID = 256
TOK = 128
CAP = 10
ROWS = 8 * CAP
RET = 32

PLACE = {7: 0, 1: 1, 6: 2, 2: 3, 5: 4, 3: 5, 4: 6, 0: 7}
OWN = slice(PLACE[0] * ROWS, PLACE[0] * ROWS + ROWS)
ORDER = (1, 7, 2, 6, 3, 5, 4)


def dot(a, b):
    return lax.dot_general(a, b, (((1,), (0,)), ((), ())), preferred_element_type=F32)


def dot_nt(a, b):
    return lax.dot_general(a, b, (((1,), (1,)), ((), ())), preferred_element_type=F32)


def dot_tn(a, b):
    return lax.dot_general(a, b, (((0,), (0,)), ((), ())), preferred_element_type=F32)


def iota(shape, dim):
    return lax.broadcasted_iota(jnp.int32, shape, dim)


def kernel(
    tok, gout, ids, gate, win, wout,
    gtok_o, ggate_o, own_io, own_oo, fin_li, fin_lo, fin_ri, fin_ro,
    raw, meta, meta_far, ms, mr, xs, ds, xo, do,
    wi, wo, act, dpre, dtacc, gacc, dt, rb, gp, gr,
    dwi, dwo, yri, yro, own_i, own_o,
    pack, rets, retr,
    core_s, core_r, loc_s, xs_s, xs_r, zx_s, zx_r, zf_s, zo_s, ya_s, ya_r,
    zb_s, zb_r, gt_s, gt_r, yb_s, yb_r, rt_s, rt_r, out_s,
):
    dp, ex = lax.axis_index("dp"), lax.axis_index("expert")
    zl, y = dp // 4, dp % 4
    zh, x, c = ex // 8, (ex // 2) % 4, ex % 2
    z = zh * 4 + zl

    def dev(dz=0, dy=0, dx=0, dc=0):
        zz, yy, xx, cc = (z + dz + 8) % 8, (y + dy + 4) % 4, (x + dx + 4) % 4, (c + dc) % 2
        return ((zz % 4) * 4 + yy, (zz // 4) * 8 + xx * 2 + cc)

    def remote(src, dst, send, recv, to):
        return pltpu.make_async_remote_copy(
            src_ref=src, dst_ref=dst, send_sem=send, recv_sem=recv, device_id=to, device_id_type=MESH
        )

    barrier = pltpu.get_barrier_semaphore()
    partners = [dev(dz=k) for k in range(1, 8)] + [dev(dy=1), dev(dy=3)]
    partners += [dev(dx=k, dc=j) for k in range(4) for j in range(2) if k or j]
    for to in partners:
        pl.semaphore_signal(barrier, inc=1, device_id=to, device_id_type=MESH)
    pl.semaphore_wait(barrier, len(partners))

    sent = []

    def start(copy):
        copy.start()
        sent.append(copy)
        return copy

    right, left = dev(dy=1), dev(dy=3)

    def y_gather(e, kind):
        src = {
            "i_r": (win.at[e], wi.at[e, 3], right, 0),
            "o_r": (wout.at[e], wo.at[e, 3], right, 1),
            "i_l": (win.at[e], wi.at[e, 1], left, 2),
            "o_l": (wout.at[e], wo.at[e, 1], left, 3),
            "i_f": (wi.at[e, 3], wi.at[e, 2], right, 4),
            "o_f": (wo.at[e, 1], wo.at[e, 2], left, 5),
        }[kind]
        return remote(src[0], src[1], ya_s.at[e, src[3]], ya_r.at[e, src[3]], src[2])

    def y_own(e, kinds):
        for kind in kinds:
            start(y_gather(e, kind))

    def y_forward(e):
        y_gather(e, "i_r").wait_recv()
        start(y_gather(e, "i_f"))
        y_gather(e, "o_l").wait_recv()
        start(y_gather(e, "o_f"))

    def y_rest(e):
        for kind in ("o_r", "i_l", "i_f", "o_f"):
            y_gather(e, kind).wait_recv()

    meta[...] = jnp.concatenate([ids[...].astype(F32), gate[...].astype(F32), jnp.zeros((4, TOK), F32)], axis=0)
    core = dev(dc=1)
    swaps = [
        remote(meta, meta_far, core_s.at[0], core_r.at[0], core),
        remote(tok, raw.at[pl.ds(TOK, TOK)], core_s.at[1], core_r.at[1], core),
        remote(gout, raw.at[pl.ds(3 * TOK, TOK)], core_s.at[2], core_r.at[2], core),
    ]
    for copy in swaps:
        start(copy)
    y_own(0, ("i_r", "o_l"))
    local = []
    for e in range(2):
        local.append(pltpu.make_async_copy(win.at[e], wi.at[e, 0], loc_s.at[e, 0]))
        local.append(pltpu.make_async_copy(wout.at[e], wo.at[e, 0], loc_s.at[e, 1]))
    for copy in local:
        copy.start()

    raw[0:TOK, :] = tok[...]
    raw[2 * TOK : 3 * TOK, :] = gout[...]
    before = (iota((TOK, TOK), 0) < iota((TOK, TOK), 1)).astype(F32).astype(BF)

    def ranks(ids0, ids1, wanted):
        hit0, hit1 = ids0 == wanted, ids1 == wanted
        hit = jnp.where(hit0 | hit1, 1.0, 0.0)
        return hit, dot(hit.astype(BF), before), hit0, hit1

    swaps[0].wait_recv()
    k = iota((16, TOK), 0)
    k_x, k_zone, k_e = (x + (k >> 2)) & 3, (zh + (k & 1)) & 1, (k >> 1) & 1
    wanted = ((k_zone * 8 + k_x * 2 + c) * 2 + k_e).astype(F32)
    codes, gates = [], []
    for side, m in enumerate((meta, meta_far)):
        hit, rank, h0, h1 = ranks(m[0:1, :], m[1:2, :], wanted)
        codes.append(jnp.where(hit > 0.0, rank + side * CAP, -1.0))
        gates.append(jnp.where(h0, m[2:3, :], 0.0) + jnp.where(h1, m[3:4, :], 0.0))
    code = jnp.concatenate(codes, axis=1).astype(jnp.int32)
    weight = jnp.concatenate(gates, axis=1)

    def x_send(part, k):
        return remote(
            ms.at[part, pl.ds(k * 80, 80)], mr.at[part, pl.ds((4 - k) % 4 * 80, 80)],
            xs_s.at[part, k], xs_r.at[part, k], dev(dx=k),
        )

    def dispatch(part):
        blocks = []
        for k in range(16):
            same = iota((20, 2 * TOK), 0) == code[k : k + 1, :]
            blocks.append(jnp.where(same, weight[k : k + 1, :] if part else 1.0, 0.0))
        spread = jnp.concatenate(blocks, axis=0).astype(BF)
        rows = dot(spread, raw[part * 2 * TOK : (part + 1) * 2 * TOK, :]).astype(BF)
        ms[part] = rows
        for k in (1, 3, 2):
            start(x_send(part, k))
        mr[part, 0:80, :] = rows[0:80, :]

    swaps[1].wait_recv()
    dispatch(0)
    swaps[2].wait_recv()
    dispatch(1)
    y_own(0, ("o_r", "i_l"))
    gp[...] = jnp.zeros_like(gp)

    number = iota((32, TOK), 0)
    own0, own1 = meta[0:1, :], meta[1:2, :]
    _, own_rank, hit0, hit1 = ranks(own0, own1, number.astype(F32))
    num_ex = number >> 1
    xr = (((num_ex >> 1) & 3) - x + 4) & 3
    cr = (num_ex + c) & 1
    zr = ((num_ex >> 3) + zh) & 1
    message = (number & 1) * (8 * RET) + (xr * 2 + cr) * RET
    row_code = (message + zr * 10).astype(F32) + own_rank
    gate_code = (message + 20 + zr).astype(F32)
    lane_code = (((4 - xr) & 3) * 20 + cr * 10).astype(F32) + own_rank

    def pick(hit, table):
        return jnp.sum(jnp.where(hit, table, 0.0), axis=0, keepdims=True).astype(jnp.int32)

    home = [[pick(hit, t) for t in (row_code, gate_code, lane_code)] for hit in (hit0, hit1)]

    o, i = iota((320, 320), 0), iota((320, 320), 1)
    oa, ia = o // 20, i // 20
    unpack = ((o - oa * 20 == i - ia * 20) & ((oa & 3) == (ia >> 2)) & ((oa >> 2) == (ia & 3)))
    unpack = unpack.astype(F32).astype(BF)

    def arrive(part):
        for k in (1, 3, 2):
            x_send(part, k).wait_recv()
        rows = dot(unpack, mr[part]).astype(BF)
        mine, theirs = (xs, ds)[part], (xo, do)[part]
        for e in range(2):
            mine[e, OWN, :] = rows[e * 160 : e * 160 + 80, :]
            theirs[e] = rows[e * 160 + 80 : e * 160 + 160, :]

    def place(at):
        return pl.ds(at * ROWS, ROWS)

    def z_copy(e, part, src, at, to, send):
        where = (xs, ds)[part]
        return remote(src, where.at[e, place(at)], send, zx_r.at[e, part, at], to)

    cond_sent = []

    def z_own(e, busy, parts=(0, 1)):
        def send(cond, copy):
            cond_sent.append((cond, copy))
            pl.when(cond)(copy.start)

        for part in parts:
            mine, theirs = (xs, ds)[part].at[e, place(PLACE[0])], (xo, do)[part].at[e]

            def go(way, rho, dz):
                return z_copy(e, part, mine, PLACE[rho], dev(dz=dz), zx_s.at[e, part, way])

            inner = (zl == 1) | (zl == 2)
            at = jnp.where(zl == 0, PLACE[1], jnp.where(zl == 1, PLACE[2], jnp.where(zl == 2, PLACE[6], PLACE[7])))
            hop = jnp.where(zl < 2, 7 - zl, 4 - zl)
            send(zl == 2 if busy else zl < 2, go(0, 7, 1))
            send(zl == 1 if busy else zl > 1, go(1, 1, 7))
            send(inner if busy else ~inner, z_copy(e, part, theirs, at, dev(dz=hop), zo_s.at[e, part]))

    def is_right(rho):
        return zl >= 6 - rho

    def z_waits(e, rhos, parts=(0, 1)):
        for rho in rhos:
            at = PLACE[rho]
            for part in parts:
                here = (xs, ds)[part].at[e, place(at)]
                z_copy(e, part, here, at, dev(dz=1), zf_s.at[e, part, at]).wait_recv()

    def z_on(e, rho, part):
        at = PLACE[rho]
        goes_right = is_right(rho)
        forward = jnp.where(goes_right, zl < 3, zl > 0)
        there = jnp.where(goes_right, PLACE[rho - 1], PLACE[(rho + 1) % 8])
        to = dev(dz=jnp.where(goes_right, 1, 7))
        return forward, z_copy(e, part, (xs, ds)[part].at[e, place(at)], there, to, zf_s.at[e, part, at])

    def z_passes(e, rhos, parts=(0, 1)):
        for rho in rhos:
            for part in parts:
                z_waits(e, (rho,), (part,))
                forward, on = z_on(e, rho, part)
                pl.when(forward)(on.start)

    ones = jnp.ones((8, HID), F32)

    def compute(e, g):
        at = pl.ds(pl.multiple_of(g * 2 * ROWS, 2 * ROWS), 2 * ROWS)
        dtacc[...] = jnp.zeros_like(dtacc)
        gacc[...] = jnp.zeros_like(gacc)

        def shard(j, _):
            w_in = wi[e, j]
            pre = dot(xs[e, at, :], w_in)
            up = dot_nt(ds[e, at, :], wo[e, j])
            sq = pre * pre
            s = jnp.tanh(GELU_SCALE * (pre + GELU_CUBIC * sq * pre))
            half = 0.5 * (1.0 + s)
            a = (pre * half).astype(BF)
            slope = half + 0.5 * pre * (1.0 - s * s) * GELU_SCALE * (1.0 + 3.0 * GELU_CUBIC * sq)
            d = (up * slope).astype(BF)
            act[j, at, :] = a
            dpre[j, at, :] = d
            gacc[...] += a.astype(F32) * up
            dtacc[...] += dot_nt(d, w_in)
            return 0

        lax.fori_loop(0, 4, shard, 0)
        dt[e, at, :] = dtacc[...].astype(BF)
        for k in range(2):
            sums = lax.dot_general(
                ones, gacc[k * ROWS : (k + 1) * ROWS, :], (((1,), (1,)), ((), ())),
                precision=lax.Precision.HIGHEST, preferred_element_type=F32,
            )
            gp[e, 2 * g + k, :, 0:ROWS] = sums

    def y_scatter(e, kind):
        src = {
            "i_2": (dwi.at[e, 2], yri.at[e], right, 0),
            "o_2": (dwo.at[e, 2], yro.at[e], left, 1),
            "o_1": (dwo.at[e, 1], fin_lo.at[e], right, 2),
            "i_3": (dwi.at[e, 3], fin_ri.at[e], left, 3),
            "i_1": (dwi.at[e, 1], fin_li.at[e], right, 4),
            "o_3": (dwo.at[e, 3], fin_ro.at[e], left, 5),
        }[kind]
        return remote(src[0], src[1], yb_s.at[e, src[3]], yb_r.at[e, src[3]], src[2])

    def weight_grads(e, j):
        def tile(t, _):
            cols = pl.ds(pl.multiple_of(t * 256, 256), 256)
            g_in, g_out = dot_tn(xs[e, :, cols], dpre[j]), dot_tn(act[j], ds[e, :, cols])
            if j:
                dwi[e, j, cols, :] = g_in.astype(BF)
                dwo[e, j, :, cols] = g_out.astype(BF)
            else:
                own_i[e, cols, :] = g_in
                own_o[e, :, cols] = g_out
            return 0

        lax.fori_loop(0, 4, tile, 0)
        for kind in {2: ("i_2", "o_2"), 1: ("o_1",), 3: ("i_3",), 0: ()}[j]:
            start(y_scatter(e, kind))
        if j == 0:
            for k, (a, b) in enumerate(((own_i, own_io), (own_o, own_oo))):
                copy = pltpu.make_async_copy(a.at[e], b.at[e], out_s.at[e, k])
                copy.start()
                outs.append(copy)

    outs = []

    def y_relay(e):
        y_scatter(e, "i_2").wait_recv()
        dwi[e, 1] = (dwi[e, 1].astype(F32) + yri[e].astype(F32)).astype(BF)
        start(y_scatter(e, "i_1"))
        y_scatter(e, "o_2").wait_recv()
        dwo[e, 3] = (dwo[e, 3].astype(F32) + yro[e].astype(F32)).astype(BF)
        start(y_scatter(e, "o_3"))

    def y_final(e):
        for kind in ("o_1", "i_3", "i_1", "o_3"):
            y_scatter(e, kind).wait_recv()

    def z_back(e, rho):
        spot = jnp.where(rho >= 5, 14 - 2 * rho, jnp.where(rho == 4, 6, 2 * rho - 1))
        at = pl.ds(pl.multiple_of(spot * ROWS, ROWS), ROWS)
        goes_right = is_right(rho)
        incoming = jnp.where(goes_right, zl < 3, zl > 0)
        first = jnp.where(goes_right, zl == 0, zl == 3)
        slot = jnp.where(first, 9, jnp.where(goes_right, rho + 1, rho - 1))
        hop = jnp.where(first, rho, jnp.where(goes_right, 7, 1))
        here = dt.at[e, at]

        @pl.when(incoming)
        def _():
            remote(here, rb.at[e, rho], zb_s.at[e, rho], zb_r.at[e, rho], dev(dz=1)).wait_recv()
            dt[e, at, :] = (dt[e, at, :].astype(F32) + rb[e, rho].astype(F32)).astype(BF)

        remote(here, rb.at[e, slot], zb_s.at[e, rho], zb_r.at[e, slot], dev(dz=hop)).start()

    edge = (zl == 0) | (zl == 3)

    def back_edge(e, pairs):
        for at_0, at_3 in pairs:
            pl.when(edge)(lambda: z_back(e, jnp.where(zl == 0, at_0, at_3)))

    def back_inner(e, pairs):
        for at_1, at_2 in pairs:
            pl.when(~edge)(lambda: z_back(e, jnp.where(zl == 1, at_1, at_2)))

    inner_first = ((1, 7), (2, 6), (7, 5), (6, 1))
    inner_last = ((3, 4), (4, 2), (5, 3))
    edge_last = ((7, 1), (6, 2))

    def z_home(e):
        own = dt.at[e, place(PLACE[0])]
        dtacc[0:ROWS, :] = dt[e, OWN, :].astype(F32)
        for cond, slot in ((zl < 3, 8), (zl > 0, 0)):

            @pl.when(cond)
            def _(slot=slot):
                remote(own, rb.at[e, slot], zb_s.at[e, 0], zb_r.at[e, slot], dev(dz=1)).wait_recv()
                dtacc[0:ROWS, :] += rb[e, slot].astype(F32)

        pack[0:ROWS, :] = dtacc[0:ROWS, :].astype(BF)
        remote(own, rb.at[e, 9], zb_s.at[e, 0], zb_r.at[e, 9], dev(dz=1)).wait_recv()
        pack[ROWS : 2 * ROWS, :] = rb[e, 9]

    def gate_copy(e, rho):
        return remote(
            gp.at[e, PLACE[rho]], gr.at[e, 8 - rho], gt_s.at[e, rho], gt_r.at[e, 8 - rho], dev(dz=rho)
        )

    def gates_out(e):
        for rho in ORDER:
            start(gate_copy(e, rho))

    peers = [(k, j) for k in (2, 1, 3, 0) for j in range(2) if k or j]

    def ret_copy(e, k, j):
        m = k * 2 + j
        n = (4 - k) % 4 * 2 + j
        return remote(
            rets.at[e, pl.ds(m * RET, RET)], retr.at[pl.ds(e * 8 * RET + n * RET, RET)],
            rt_s.at[e, m], rt_r.at[e, n], dev(dx=k, dc=j),
        )

    def give_back(e):
        z_home(e)
        own_sum, other_sum = gp[e, PLACE[0]], jnp.zeros((8, 128), F32)
        for rho in range(1, 8):
            gate_copy(e, 8 - rho).wait_recv()
            near = jnp.where(rho < 4, rho <= 3 - zl, rho >= 8 - zl)
            value = gr[e, rho]
            own_sum += jnp.where(near, value, 0.0)
            other_sum += jnp.where(near, 0.0, value)
        line = iota((16, 128), 0)
        rows = jnp.zeros((16, 128), F32)
        for at, value in enumerate((own_sum[0:1], other_sum[0:1])):
            high = value.astype(BF).astype(F32)
            rows = jnp.where(line == at, high, jnp.where(line == at + 2, value - high, rows))
        pack[160:176, :] = jnp.zeros((16, D), BF)
        pack[160:176, 0:128] = rows.astype(BF)
        o, i = iota((8 * RET, 176), 0), iota((8 * RET, 176), 1)
        m, w = o >> 5, o & 31
        q = w // 10
        source = jnp.where(w < 20, q * ROWS + m * 10 + (w - q * 10), 160 + w - 20)
        chosen = (source == i).astype(F32).astype(BF)
        rets[e] = dot(chosen, pack[...]).astype(BF)
        for k, j in peers:
            start(ret_copy(e, k, j))
        retr[e * 8 * RET : e * 8 * RET + RET, :] = rets[e, 0:RET, :]

    def last_passes(e, between):
        if e == 0:
            pl.when(~edge)(lambda: z_passes(e, (3, 5, 4), (1,)))
            z_own(1, True)
        else:
            pl.when(~edge)(lambda: z_passes(e, (3, 5, 4)))
        pl.when(edge)(lambda: z_waits(e, (4,)))
        compute(e, 3)
        back_edge(e, ((4, 4),))
        between()
        pl.when(edge)(lambda: z_waits(e, (3, 5)))
        compute(e, 2)
        back_edge(e, ((3, 5), (5, 3)))

    arrive(0)
    z_own(0, True, (0,))
    z_own(0, False, (0,))
    z_passes(0, (1, 7), (0,))
    arrive(1)
    z_own(0, True, (1,))
    z_own(0, False, (1,))
    y_forward(0)
    z_passes(0, (2, 6), (0,))
    z_passes(0, (1, 7), (1,))
    y_own(1, ("i_r", "o_l"))
    pl.when(~edge)(lambda: z_passes(0, (3, 5, 4), (0,)))
    z_passes(0, (2, 6), (1,))
    z_own(1, False)
    y_own(1, ("o_r", "i_l"))
    for copy in local:
        copy.wait()
    y_rest(0)
    compute(0, 0)
    compute(0, 1)
    back_edge(0, ((1, 7), (2, 6)))
    last_passes(0, lambda: y_forward(1))
    weight_grads(0, 2)
    weight_grads(0, 1)
    weight_grads(0, 3)
    z_passes(1, (1, 7))
    gates_out(0)
    back_inner(0, inner_first)
    z_passes(1, (2, 6))
    weight_grads(0, 0)
    y_relay(0)
    back_inner(0, inner_last)
    back_edge(0, edge_last)
    y_rest(1)
    compute(1, 0)
    compute(1, 1)
    back_edge(1, ((1, 7), (2, 6)))
    last_passes(1, lambda: give_back(0))
    weight_grads(1, 2)
    weight_grads(1, 1)
    weight_grads(1, 3)
    back_inner(1, inner_first)
    gates_out(1)
    back_inner(1, inner_last)
    back_edge(1, edge_last)
    weight_grads(1, 0)
    y_relay(1)
    give_back(1)
    y_final(0)
    for e in range(2):
        for k, j in peers:
            ret_copy(e, k, j).wait_recv()
    line = iota((16 * RET, TOK), 0)
    both = (line == home[0][0]) | (line == home[1][0])
    gtok_o[...] = dot_tn(both.astype(F32).astype(BF), retr[...]).astype(BF)
    for k in range(2):
        gate_row, lane = home[k][1], home[k][2]
        rows_of = ((line == gate_row) | (line == gate_row + 2)).astype(F32).astype(BF)
        found = dot_tn(retr[:, 0:128], rows_of)
        value = jnp.sum(jnp.where(iota((128, TOK), 0) == lane, found, 0.0), axis=0, keepdims=True)
        ggate_o[k : k + 1, :] = value / meta[2 + k : 3 + k, :]
    y_final(1)
    for copy in sent:
        copy.wait_send()
    cond_sent += [z_on(e, rho, part) for e in range(2) for rho in ORDER for part in range(2)]
    for cond, copy in cond_sent:
        pl.when(cond)(copy.wait_send)
    for e in range(2):
        for rho in range(1, 8):
            remote(dt.at[e, place(0)], rb.at[e, rho], zb_s.at[e, rho], zb_r.at[e, rho], dev(dz=1)).wait_send()
    for copy in outs:
        copy.wait()


def per_device(tokens, grad_out, expert_ids, gate_values, weight_in, weight_out):
    v, dma = pltpu.VMEM, pltpu.SemaphoreType.DMA
    scratch = [
        v((4 * TOK, D), BF), v((8, TOK), F32), v((8, TOK), F32), v((2, 320, D), BF), v((2, 320, D), BF),
        v((2, 640, D), BF), v((2, 640, D), BF), v((2, ROWS, D), BF), v((2, ROWS, D), BF),
        v((2, 4, D, HID), BF), v((2, 4, HID, D), BF), v((4, 640, HID), BF), v((4, 640, HID), BF),
        v((2 * ROWS, D), F32), v((2 * ROWS, HID), F32), v((2, 640, D), BF), v((2, 10, ROWS, D), BF),
        v((2, 8, 8, 128), F32), v((2, 8, 8, 128), F32),
        v((2, 4, D, HID), BF), v((2, 4, HID, D), BF), v((2, D, HID), BF), v((2, HID, D), BF),
        v((2, D, HID), F32), v((2, HID, D), F32),
        v((176, D), BF), v((2, 8 * RET, D), BF), v((16 * RET, D), BF),
        dma((3,)), dma((3,)), dma((2, 2)), dma((2, 4)), dma((2, 4)),
        dma((2, 2, 2)), dma((2, 2, 8)), dma((2, 2, 8)), dma((2, 2)), dma((2, 6)), dma((2, 6)),
        dma((2, 8)), dma((2, 10)), dma((2, 8)), dma((2, 8)), dma((2, 6)), dma((2, 6)), dma((2, 8)), dma((2, 8)),
        dma((2, 2)),
    ]
    vm, hbm = pl.BlockSpec(memory_space=pltpu.VMEM), pl.BlockSpec(memory_space=pl.ANY)
    shapes = [((TOK, D), BF), ((2, TOK), F32), ((2, D, HID), F32), ((2, HID, D), F32)]
    shapes += [((2, D, HID), BF), ((2, HID, D), BF)] * 2
    gtok, ggate, own_i, own_o, left_i, left_o, right_i, right_o = pl.pallas_call(
        kernel,
        out_shape=[jax.ShapeDtypeStruct(*of) for of in shapes],
        in_specs=[vm, vm, vm, vm, hbm, hbm],
        out_specs=[vm, vm, hbm, hbm, hbm, hbm, hbm, hbm],
        scratch_shapes=scratch,
        compiler_params=pltpu.CompilerParams(
            collective_id=0, has_side_effects=True, vmem_limit_bytes=62 * 2**20
        ),
        name="moe_backward",
    )(tokens, grad_out, expert_ids.T, gate_values.T, weight_in, weight_out)
    gwin = own_i + left_i.astype(F32) + right_i.astype(F32)
    gwout = own_o + left_o.astype(F32) + right_o.astype(F32)
    return gtok, ggate.T, gwin, gwout


def solution(mesh):
    placed = (
        P(("dp", "expert"), None),
        P(("dp", "expert"), None),
        P(("dp", "expert"), None),
        P(("dp", "expert"), None),
        P("expert", None, "dp"),
        P("expert", "dp", None),
    )
    return jax.shard_map(
        per_device,
        mesh=mesh,
        in_specs=placed,
        out_specs=(
            P(("dp", "expert"), None),
            P(("dp", "expert"), None),
            P("expert", None, "dp"),
            P("expert", "dp", None),
        ),
        check_vma=False,
    )
```
